512 devices in a mesh: gx: 2 (over core), yz: 64 (over x, z, y_hi), ta: 4 (over y_lo).
Axes of the slice: x: 4, y: 8 (y_hi: 2, y_lo: 4; y = y_hi * 4 + y_lo), z: 8, core: 2. Of those that a mesh axis runs over, the one named last changes fastest.
Arguments:
- snapshot: bfloat16 [1024, 512, 8, 256], P('gx', 'yz', 'ta'), may hold values from -6144 to 6144
- y_factor: bfloat16 [512, 256], P('yz'), may hold values from -0.5 to 2.5
- z_factor: bfloat16 [256, 256], P('yz'), may hold values from -0.5 to 2.5
- t_factor: bfloat16 [8, 256], P('ta'), may hold values from -0.5 to 2.5
Outputs:
- x_factor: float32 [1024, 256], P(('gx', 'yz', 'ta'))
The draws below stay inside these ranges and needn't reach their ends.
All inputs are finite; a program needn't handle non-finite values.
Results may differ from the reference program's by a relative error of at most 0.0003.
Values may be sent and summed in bfloat16 or wider, within the bound.
No kernel may reach another device: no remote copies, remote signals or barrier semaphores. Data moves between devices by JAX's collectives and lax.ppermute only.
A program may use at most 64 MiB of HBM per device.

```python
import jax
import jax.numpy as jnp
from jax import lax

RANK = 256
K = 256
I = 1024
J = 512
L = 8


def steps_of(own_key, extent, split, low, high):
    level, own = 1.0, jax.random.fold_in(own_key, 6)
    for position, blocks in split:
        heights = jnp.exp(jax.random.uniform(jax.random.fold_in(own, position), (blocks,), jnp.float32, low / len(split), high / len(split)))
        level = level * jnp.repeat(heights, extent[position] // blocks).reshape([-1 if axis == position else 1 for axis in range(len(extent))])
    return level


def scatter_about(own_key, dims, width, bound, shards=(), held_as=jnp.bfloat16):
    array = width * jax.random.normal(own_key, dims, jnp.float32)
    if shards:
        array = array * steps_of(own_key, dims, shards, -0.22, 0.18)
    return jnp.clip(array, -bound, bound).astype(held_as)


def setup_inputs(seed: int = 0) -> dict:
    arg_keys = jax.random.split(jax.random.key(seed), 5)
    snapshot = scatter_about(arg_keys[0], (I, J, L, K), 1024.0, 6144.0, ((0, 2), (1, 64), (2, 4)))
    y_factor = jnp.clip(-0.5 + 3.0 * jax.random.uniform(arg_keys[1], (J, RANK), jnp.float32) ** steps_of(arg_keys[1], (J, RANK), ((0, 64),), -0.2, 0.2), -0.5, 2.5).astype(jnp.bfloat16)
    z_factor = jnp.clip(-0.5 + 3.0 * jax.random.uniform(arg_keys[2], (K, RANK), jnp.float32) ** steps_of(arg_keys[2], (K, RANK), ((0, 64),), -0.2, 0.2), -0.5, 2.5).astype(jnp.bfloat16)
    t_factor = jnp.clip(-0.5 + 3.0 * jax.random.uniform(arg_keys[3], (L, RANK), jnp.float32) ** steps_of(arg_keys[3], (L, RANK), ((0, 4),), -0.2, 0.2), -0.5, 2.5).astype(jnp.bfloat16)
    return {"snapshot": snapshot, "y_factor": y_factor, "z_factor": z_factor, "t_factor": t_factor}


def reference(snapshot, y_factor, z_factor, t_factor):
    weights = (y_factor.astype(jnp.float32)[:, None, :] * t_factor.astype(jnp.float32)[None, :, :]).reshape(J * L, RANK)
    blocks = snapshot.reshape(I // 64, 64 * J * L, K)

    def one_block(block):
        contracted = jnp.dot(block.astype(jnp.float32), z_factor.astype(jnp.float32), preferred_element_type=jnp.float32).reshape(64, J * L, RANK)
        return jnp.sum(contracted * weights[None], axis=1)
    mttkrp = lax.map(one_block, blocks).reshape(I, RANK)
    gram_y = jnp.dot(y_factor.T.astype(jnp.float32), y_factor.astype(jnp.float32), preferred_element_type=jnp.float32)
    gram_z = jnp.dot(z_factor.T.astype(jnp.float32), z_factor.astype(jnp.float32), preferred_element_type=jnp.float32)
    gram_t = jnp.dot(t_factor.T.astype(jnp.float32), t_factor.astype(jnp.float32), preferred_element_type=jnp.float32)
    normal_matrix = gram_y * gram_z * gram_t
    lower = jnp.linalg.cholesky(normal_matrix)
    return jax.scipy.linalg.cho_solve((lower, True), mttkrp.T).T
```

```python
import jax
import jax.numpy as jnp
from jax import lax
from jax.experimental import pallas as pl
from jax.experimental.pallas import tpu as pltpu
from jax.sharding import PartitionSpec as P

SUB = 8
SUPER = 32
TILE = 128
CONTRACT_LAST = (((1,), (0,)), ((), ()))
CONTRACT_ROWS = (((0,), (0,)), ((), ()))


def three_parts(values):
    high = values.astype(jnp.bfloat16)
    rest = values - high.astype(jnp.float32)
    middle = rest.astype(jnp.bfloat16)
    low = (rest - middle.astype(jnp.float32)).astype(jnp.bfloat16)
    return high, middle, low


def product_over_rows(left, right):
    left_high, left_middle, left_low = three_parts(left)
    right_high, right_middle, right_low = three_parts(right)
    lefts = jnp.concatenate([left_high, left_high, left_middle, left_high, left_low, left_middle], axis=0)
    rights = jnp.concatenate([right_high, right_middle, right_high, right_low, right_high, right_middle], axis=0)
    return lax.dot_general(lefts, rights, CONTRACT_ROWS, preferred_element_type=jnp.float32)


def inverse_cholesky_factor(matrix):
    rank = matrix.shape[0]
    lane = lax.broadcasted_iota(jnp.int32, (SUB, rank), 1)
    row = lax.broadcasted_iota(jnp.int32, (SUB, rank), 0)
    narrow_row = lax.broadcasted_iota(jnp.int32, (SUB, 128), 0)
    wide_lane = lax.broadcasted_iota(jnp.int32, (SUPER, rank), 1)
    wide_row = lax.broadcasted_iota(jnp.int32, (SUPER, rank), 0)
    wide = rank // 128
    rows = [matrix[start : start + SUB, :] for start in range(0, rank, SUB)]
    blocks = SUPER // SUB
    for first in range(0, rank, SUPER):
        panel = rows[first // SUB : first // SUB + blocks]
        for block in range(blocks):
            start = first + block * SUB
            below = range(block, blocks)
            column = {
                (j, i): jnp.broadcast_to(panel[i][:, start + j : start + j + 1], (SUB, 128))
                for j in range(SUB)
                for i in below
            }
            own = (lane >= start) & (lane < start + SUB)
            for i in below:
                identity = jnp.where(lane - start == row, 1.0, 0.0) if i == block else 0.0
                panel[i] = jnp.where(own, identity, panel[i])
            scale = None
            for j in range(SUB):
                pivot = jnp.broadcast_to(column[j, block][j : j + 1, :], (SUB, 128))
                root = lax.rsqrt(pivot)
                inverse = 1.0 / pivot
                scale = root if scale is None else jnp.where(narrow_row == j, root, scale)
                factor = {i: column[j, i] * inverse for i in below}
                if j == SUB - 1:
                    factor.pop(block)
                else:
                    factor[block] = jnp.where(narrow_row > j, factor[block], 0.0)
                for other in range(j + 1, SUB):
                    entry = jnp.broadcast_to(column[other, block][j : j + 1, :], (SUB, 128))
                    for i in factor:
                        column[other, i] = column[other, i] - factor[i] * entry
                entry = jnp.broadcast_to(panel[block][j : j + 1, :], (SUB, rank))
                for i in factor:
                    panel[i] = panel[i] - jnp.concatenate([factor[i]] * wide, axis=1) * entry
            panel[block] = panel[block] * jnp.concatenate([scale] * wide, axis=1)
        rows[first // SUB : first // SUB + blocks] = panel
        end = first + SUPER
        if end < rank:
            upper = jnp.concatenate(panel, axis=0)
            done = jnp.where((wide_lane < end) & (wide_lane - first > wide_row), 0.0, upper)
            from_lane = end // 128 * 128
            update = product_over_rows(upper[:, from_lane:], done)
            fresh = (lane >= first) & (lane < end)
            for i in range(end // SUB, rank // SUB):
                at = i * SUB - from_lane
                rows[i] = jnp.where(fresh, 0.0, rows[i]) - update[at : at + SUB, :]
    kept = [jnp.where(lane <= row + i * SUB, rows[i], 0.0) for i in range(rank // SUB)]
    return jnp.concatenate(kept, axis=0)


def inverse_kernel(y_ref, other_y_ref, z_ref, t_ref, high_ref, middle_ref, low_ref):
    def gram(factor):
        return lax.dot_general(factor, factor, CONTRACT_ROWS, preferred_element_type=jnp.float32)

    gram_y = gram(y_ref[...]) + gram(other_y_ref[...])
    normal_matrix = gram_y * gram(z_ref[...]) * gram(t_ref[...])
    inverse_factor = inverse_cholesky_factor(normal_matrix)
    inverse = product_over_rows(inverse_factor, inverse_factor)
    high_ref[...], middle_ref[...], low_ref[...] = three_parts(inverse)


def contract_kernel(snapshot_ref, z_ref, y_ref, t_ref, out_ref):
    z, y, t = z_ref[...], y_ref[...], t_ref[...]
    cols_y, cols_t = y.shape[0], t.shape[0]
    group = out_ref.shape[1]
    for start in range(0, snapshot_ref.shape[1], TILE):
        total = None
        for j in range(cols_y):
            for l in range(cols_t):
                part = lax.dot_general(
                    snapshot_ref[j * cols_t + l, start : start + TILE, :],
                    z,
                    CONTRACT_LAST,
                    preferred_element_type=jnp.float32,
                )
                part = part * (y[j : j + 1, :] * t[l : l + 1, :])
                total = part if total is None else total + part
        out_ref[start // group : (start + TILE) // group] = total.reshape(TILE // group, group, total.shape[1])


def finish_kernel(parts_ref, high_ref, middle_ref, low_ref, out_ref):
    summed = jnp.sum(parts_ref[...], axis=0)
    count = summed.shape[0]
    lefts = jnp.concatenate([part.astype(jnp.float32) for part in three_parts(summed)], axis=0).astype(jnp.bfloat16)

    def product(right_ref):
        return lax.dot_general(lefts, right_ref[...], CONTRACT_LAST, preferred_element_type=jnp.float32)

    by_high, by_middle, by_low = product(high_ref), product(middle_ref), product(low_ref)
    small = by_low[:count] + by_middle[count : 2 * count] + by_high[2 * count :]
    out_ref[...] = by_high[:count] + (by_middle[:count] + by_high[count : 2 * count] + small)


def copies_kernel(z_ref, y_ref, out_ref):
    z, y = z_ref[...].astype(jnp.float32), y_ref[...].astype(jnp.float32)
    half = y.shape[0] // 2
    own_half = jnp.where(lax.axis_index("gx") == 0, y[:half], y[half:])
    rows = jnp.concatenate([z, own_half], axis=0).astype(jnp.bfloat16)
    out_ref[...] = jnp.broadcast_to(rows[None], out_ref.shape)


def kernel_call(body, out_shape, flops, bytes_accessed, vmem_mib=24):
    return pl.pallas_call(
        body,
        out_shape=out_shape,
        compiler_params=pltpu.CompilerParams(vmem_limit_bytes=vmem_mib << 20),
        cost_estimate=pl.CostEstimate(flops=flops, bytes_accessed=bytes_accessed, transcendentals=0),
    )


def gathered(y_factor, z_factor):
    steps, blocks = lax.axis_size("ta"), lax.axis_size("yz")
    rows_z, rank = z_factor.shape
    half = y_factor.shape[0] // 2
    groups = [[b * steps + (g + b % 2 * (steps // 2)) % steps for b in range(blocks)] for g in range(steps)]
    shape = jax.ShapeDtypeStruct((blocks, rows_z + half, rank), z_factor.dtype)
    copies = kernel_call(copies_kernel, shape, 0, 2 * shape.size, 60)(z_factor, y_factor)
    arrived = lax.all_to_all(copies, ("yz", "ta"), 0, 0, axis_index_groups=groups)
    return arrived[:, :rows_z].reshape(blocks * rows_z, rank), arrived[:, rows_z:].reshape(blocks * half, rank)


def per_device(snapshot, y_factor, z_factor, t_factor):
    rows_x, cols_y, cols_t, cells_z = snapshot.shape
    rank = z_factor.shape[1]
    devices = lax.axis_size(("yz", "ta"))
    own_rows = rows_x // devices
    steps = lax.axis_size("ta")

    def swapped(array, distance):
        return lax.ppermute(array, "ta", [(i, i ^ distance) for i in range(steps)])

    whole_z, half_y = gathered(y_factor, z_factor)
    t_wide = t_factor.astype(jnp.float32)
    t_pair = swapped(t_wide, 1)
    whole_z, t_pair = lax.optimization_barrier((whole_z, t_pair))
    t_pair = jnp.concatenate([t_wide, t_pair], axis=0)
    ordered = snapshot.transpose(1, 2, 0, 3).reshape(cols_y * cols_t, rows_x, cells_z)
    own_sums = jax.ShapeDtypeStruct((devices, own_rows, rank), jnp.float32)
    sums = kernel_call(contract_kernel, own_sums, 2 * snapshot.size * rank, 2 * snapshot.size)(
        ordered, whole_z, y_factor.astype(jnp.float32), t_wide
    )
    parts = lax.all_to_all(sums, ("yz", "ta"), 0, 0)
    other_y = lax.ppermute(half_y, "gx", [(0, 1), (1, 0)])
    whole_t = jnp.concatenate([t_pair, swapped(t_pair, 2)], axis=0)
    whole_t = jnp.concatenate([whole_t, jnp.zeros_like(whole_t)], axis=0).astype(jnp.bfloat16)
    square = jax.ShapeDtypeStruct((rank, rank), jnp.bfloat16)
    inverse = kernel_call(inverse_kernel, [square] * 3, 100_000_000, 1_000_000)(half_y, other_y, whole_z, whole_t)
    own = jax.ShapeDtypeStruct((own_rows, rank), jnp.float32)
    return kernel_call(finish_kernel, own, 6 * rank * rank, 4 * rows_x * rank)(parts, *inverse)


def solution(mesh):
    return jax.shard_map(
        per_device,
        mesh=mesh,
        in_specs=(P("gx", "yz", "ta", None), P("yz", None), P("yz", None), P("ta", None)),
        out_specs=P(("gx", "yz", "ta"), None),
        check_vma=False,
    )
```

```python
import jax
import jax.numpy as jnp
from jax import lax
from jax.experimental import pallas as pl
from jax.experimental.pallas import tpu as pltpu
from jax.sharding import PartitionSpec as P

SUB = 8
SUPER = 32
TILE = 128
CONTRACT_LAST = (((1,), (0,)), ((), ()))
CONTRACT_ROWS = (((0,), (0,)), ((), ()))


def three_parts(values):
    high = values.astype(jnp.bfloat16)
    rest = values - high.astype(jnp.float32)
    middle = rest.astype(jnp.bfloat16)
    low = (rest - middle.astype(jnp.float32)).astype(jnp.bfloat16)
    return high, middle, low


def product_over_rows(left, right):
    left_high, left_middle, left_low = three_parts(left)
    right_high, right_middle, right_low = three_parts(right)
    lefts = jnp.concatenate([left_high, left_high, left_middle, left_high, left_low, left_middle], axis=0)
    rights = jnp.concatenate([right_high, right_middle, right_high, right_low, right_high, right_middle], axis=0)
    return lax.dot_general(lefts, rights, CONTRACT_ROWS, preferred_element_type=jnp.float32)


def inverse_cholesky_factor(matrix):
    rank = matrix.shape[0]
    lane = lax.broadcasted_iota(jnp.int32, (SUB, rank), 1)
    row = lax.broadcasted_iota(jnp.int32, (SUB, rank), 0)
    narrow_row = lax.broadcasted_iota(jnp.int32, (SUB, 128), 0)
    wide_lane = lax.broadcasted_iota(jnp.int32, (SUPER, rank), 1)
    wide_row = lax.broadcasted_iota(jnp.int32, (SUPER, rank), 0)
    wide = rank // 128
    rows = [matrix[start : start + SUB, :] for start in range(0, rank, SUB)]
    blocks = SUPER // SUB
    for first in range(0, rank, SUPER):
        panel = rows[first // SUB : first // SUB + blocks]
        for block in range(blocks):
            start = first + block * SUB
            below = range(block, blocks)
            column = {
                (j, i): jnp.broadcast_to(panel[i][:, start + j : start + j + 1], (SUB, 128))
                for j in range(SUB)
                for i in below
            }
            own = (lane >= start) & (lane < start + SUB)
            for i in below:
                identity = jnp.where(lane - start == row, 1.0, 0.0) if i == block else 0.0
                panel[i] = jnp.where(own, identity, panel[i])
            scale = None
            for j in range(SUB):
                pivot = jnp.broadcast_to(column[j, block][j : j + 1, :], (SUB, 128))
                root = lax.rsqrt(pivot)
                inverse = 1.0 / pivot
                scale = root if scale is None else jnp.where(narrow_row == j, root, scale)
                factor = {i: column[j, i] * inverse for i in below}
                if j == SUB - 1:
                    factor.pop(block)
                else:
                    factor[block] = jnp.where(narrow_row > j, factor[block], 0.0)
                for other in range(j + 1, SUB):
                    entry = jnp.broadcast_to(column[other, block][j : j + 1, :], (SUB, 128))
                    for i in factor:
                        column[other, i] = column[other, i] - factor[i] * entry
                entry = jnp.broadcast_to(panel[block][j : j + 1, :], (SUB, rank))
                for i in factor:
                    panel[i] = panel[i] - jnp.concatenate([factor[i]] * wide, axis=1) * entry
            panel[block] = panel[block] * jnp.concatenate([scale] * wide, axis=1)
        rows[first // SUB : first // SUB + blocks] = panel
        end = first + SUPER
        if end < rank:
            upper = jnp.concatenate(panel, axis=0)
            done = jnp.where((wide_lane < end) & (wide_lane - first > wide_row), 0.0, upper)
            from_lane = end // 128 * 128
            update = product_over_rows(upper[:, from_lane:], done)
            fresh = (lane >= first) & (lane < end)
            for i in range(end // SUB, rank // SUB):
                at = i * SUB - from_lane
                rows[i] = jnp.where(fresh, 0.0, rows[i]) - update[at : at + SUB, :]
    kept = [jnp.where(lane <= row + i * SUB, rows[i], 0.0) for i in range(rank // SUB)]
    return jnp.concatenate(kept, axis=0)


def inverse_kernel(y_ref, other_y_ref, z_ref, t_ref, high_ref, middle_ref, low_ref):
    def gram(factor):
        return lax.dot_general(factor, factor, CONTRACT_ROWS, preferred_element_type=jnp.float32)

    gram_y = gram(y_ref[...]) + gram(other_y_ref[...])
    normal_matrix = gram_y * gram(z_ref[...]) * gram(t_ref[...])
    inverse_factor = inverse_cholesky_factor(normal_matrix)
    inverse = product_over_rows(inverse_factor, inverse_factor)
    high_ref[...], middle_ref[...], low_ref[...] = three_parts(inverse)


def contract_kernel(snapshot_ref, z_ref, y_ref, t_ref, out_ref, held, arrived):
    rows_x = snapshot_ref.shape[1]
    copies = []
    for index, start in enumerate(range(0, rows_x, TILE)):
        rows = pl.ds(start, TILE)
        copies.append(pltpu.make_async_copy(snapshot_ref.at[:, rows], held.at[:, rows], arrived.at[index]))
        copies[-1].start()
    z, y, t = z_ref[...], y_ref[...].astype(jnp.float32), t_ref[...].astype(jnp.float32)
    cols_y, cols_t = y.shape[0], t.shape[0]
    group = out_ref.shape[1]
    for copy, start in zip(copies, range(0, rows_x, TILE)):
        copy.wait()
        total = None
        for j in range(cols_y):
            for l in range(cols_t):
                part = lax.dot_general(
                    held[j * cols_t + l, start : start + TILE, :],
                    z,
                    CONTRACT_LAST,
                    preferred_element_type=jnp.float32,
                )
                part = part * (y[j : j + 1, :] * t[l : l + 1, :])
                total = part if total is None else total + part
        out_ref[start // group : (start + TILE) // group] = total.reshape(TILE // group, group, total.shape[1])


def finish_kernel(parts_ref, high_ref, middle_ref, low_ref, out_ref):
    summed = jnp.sum(parts_ref[...], axis=0)
    count = summed.shape[0]
    lefts = jnp.concatenate([part.astype(jnp.float32) for part in three_parts(summed)], axis=0).astype(jnp.bfloat16)

    def product(right_ref):
        return lax.dot_general(lefts, right_ref[...], CONTRACT_LAST, preferred_element_type=jnp.float32)

    by_high, by_middle, by_low = product(high_ref), product(middle_ref), product(low_ref)
    small = by_low[:count] + by_middle[count : 2 * count] + by_high[2 * count :]
    out_ref[...] = by_high[:count] + (by_middle[:count] + by_high[count : 2 * count] + small)


def copies_kernel(z_ref, y_ref, out_ref):
    z, y = z_ref[...].astype(jnp.float32), y_ref[...].astype(jnp.float32)
    half = y.shape[0] // 2
    own_half = jnp.where(lax.axis_index("gx") == 0, y[:half], y[half:])
    rows = jnp.concatenate([z, own_half], axis=0).astype(jnp.bfloat16)
    out_ref[...] = jnp.broadcast_to(rows[None], out_ref.shape)


def kernel_call(body, out_shape, flops, bytes_accessed, vmem_mib=24):
    return pl.pallas_call(
        body,
        out_shape=out_shape,
        compiler_params=pltpu.CompilerParams(vmem_limit_bytes=vmem_mib << 20),
        cost_estimate=pl.CostEstimate(flops=flops, bytes_accessed=bytes_accessed, transcendentals=0),
    )


def gathered(y_factor, z_factor):
    steps, blocks = lax.axis_size("ta"), lax.axis_size("yz")
    rows_z, rank = z_factor.shape
    half = y_factor.shape[0] // 2
    groups = [[b * steps + (g + b % 2 * (steps // 2)) % steps for b in range(blocks)] for g in range(steps)]
    shape = jax.ShapeDtypeStruct((blocks, rows_z + half, rank), z_factor.dtype)
    copies = kernel_call(copies_kernel, shape, 0, 2 * shape.size, 60)(z_factor, y_factor)
    arrived = lax.all_to_all(copies, ("yz", "ta"), 0, 0, axis_index_groups=groups)
    return arrived[:, :rows_z].reshape(blocks * rows_z, rank), arrived[:, rows_z:].reshape(blocks * half, rank)


def per_device(snapshot, y_factor, z_factor, t_factor):
    rows_x, cols_y, cols_t, cells_z = snapshot.shape
    rank = z_factor.shape[1]
    devices = lax.axis_size(("yz", "ta"))
    own_rows = rows_x // devices
    steps = lax.axis_size("ta")

    def swapped(array, distance):
        return lax.ppermute(array, "ta", [(i, i ^ distance) for i in range(steps)])

    whole_z, half_y = gathered(y_factor, z_factor)
    t_wide = t_factor.astype(jnp.float32)
    t_pair = swapped(t_wide, 1)
    whole_z, t_pair = lax.optimization_barrier((whole_z, t_pair))
    t_pair = jnp.concatenate([t_wide, t_pair], axis=0)
    ordered = snapshot.transpose(1, 2, 0, 3).reshape(cols_y * cols_t, rows_x, cells_z)
    in_vmem = pl.BlockSpec(memory_space=pltpu.VMEM)
    sums = pl.pallas_call(
        contract_kernel,
        in_specs=[pl.BlockSpec(memory_space=pltpu.HBM), in_vmem, in_vmem, in_vmem],
        out_specs=in_vmem,
        out_shape=jax.ShapeDtypeStruct((devices, own_rows, rank), jnp.float32),
        scratch_shapes=[
            pltpu.VMEM(ordered.shape, ordered.dtype),
            pltpu.SemaphoreType.DMA((rows_x // TILE,)),
        ],
        compiler_params=pltpu.CompilerParams(vmem_limit_bytes=52 << 20),
        cost_estimate=pl.CostEstimate(
            flops=2 * snapshot.size * rank, bytes_accessed=2 * snapshot.size, transcendentals=0
        ),
    )(ordered, whole_z, y_factor, t_factor)
    parts = lax.all_to_all(sums, ("yz", "ta"), 0, 0)
    other_y = lax.ppermute(half_y, "gx", [(0, 1), (1, 0)])
    whole_t = jnp.concatenate([t_pair, swapped(t_pair, 2)], axis=0)
    whole_t = jnp.concatenate([whole_t, jnp.zeros_like(whole_t)], axis=0).astype(jnp.bfloat16)
    square = jax.ShapeDtypeStruct((rank, rank), jnp.bfloat16)
    inverse = kernel_call(inverse_kernel, [square] * 3, 100_000_000, 1_000_000)(half_y, other_y, whole_z, whole_t)
    own = jax.ShapeDtypeStruct((own_rows, rank), jnp.float32)
    return kernel_call(finish_kernel, own, 6 * rank * rank, 4 * rows_x * rank)(parts, *inverse)


def solution(mesh):
    return jax.shard_map(
        per_device,
        mesh=mesh,
        in_specs=(P("gx", "yz", "ta", None), P("yz", None), P("yz", None), P("ta", None)),
        out_specs=P(("gx", "yz", "ta"), None),
        check_vma=False,
    )
```
